32 devices in a mesh: node: 16 (over z, x, core), ctrl: 2 (over y).
Axes of the slice: x: 2, y: 2, z: 4, core: 2. Of those that a mesh axis runs over, the one named last changes fastest.
Arguments:
- sensitivity: bfloat16 [96, 65536], P(None, 'node'), may hold values from -1.5 to 1.5
- node_xyz: float32 [3, 65536], P(None, 'node'), may hold values from 0 to 1
- ctrl_xyz: float32 [3, 16384], P(None, 'ctrl'), may hold values from 0 to 1
- inverse: bfloat16 [16384, 16384], P('ctrl', 'node'), may hold values from -0.046875 to 0.046875
Outputs:
- control_grad: float32 [96, 16384], P(None, ('node', 'ctrl'))
The draws below stay inside these ranges and needn't reach their ends.
All inputs are finite; a program needn't handle non-finite values.
Results may differ from the reference program's by a relative error of at most 0.004.
Values may be sent and summed in bfloat16 or wider, within the bound.
A program may use at most 64 MiB of HBM per device.

```python
import jax
import jax.numpy as jnp
from jax import lax

OBJ = 32
NC = 16384
NODES = 65536


def level_of(key, shape, shards, least, largest):
    gain = 1.0
    for position, blocks in shards:
        heights = jax.random.uniform(jax.random.fold_in(jax.random.fold_in(key, 6), position), (blocks,), jnp.float32, least / len(shards), largest / len(shards))
        gain = gain * jnp.repeat(jnp.exp(heights), shape[position] // blocks).reshape((-1,) + (1,) * (len(shape) - 1 - position))
    return gain


def scatter_about(stream_key, shape, width, most, shards=(), held_as=jnp.bfloat16):
    values = jax.random.normal(stream_key, shape, jnp.float32) * width
    if len(shards) > 0:
        values = level_of(stream_key, shape, shards, -0.22, 0.18) * values
    return jnp.clip(values, min=-most, max=most).astype(held_as)


def setup_inputs(seed: int = 0) -> dict:
    key_of = jax.random.split(jax.random.key(seed), 5)
    sensitivity = scatter_about(key_of[0], (3 * OBJ, NODES), (max(NODES // 4096, 1)) ** -0.5, 1.5, ((1, 16),))
    node_xyz = jnp.clip(1.0 * jax.random.uniform(key_of[1], (3, NODES), jnp.float32) ** level_of(key_of[1], (3, NODES), ((1, 16),), -0.2, 0.2), 0.0, 1.0)
    ctrl_xyz = jnp.clip(1.0 * jax.random.uniform(key_of[2], (3, NC), jnp.float32) ** level_of(key_of[2], (3, NC), ((1, 2),), -0.2, 0.2), 0.0, 1.0)
    inverse = scatter_about(key_of[3], (NC, NC), NC ** -0.5, 0.046875, ((0, 2), (1, 16)))
    return {"sensitivity": sensitivity, "node_xyz": node_xyz, "ctrl_xyz": ctrl_xyz, "inverse": inverse}


support_radius = 0.12

def kernel_tile(node_part, ctrl_xyz):
    delta_x = node_part[0][:, None] - ctrl_xyz[0][None, :]
    delta_y = node_part[1][:, None] - ctrl_xyz[1][None, :]
    delta_z = node_part[2][:, None] - ctrl_xyz[2][None, :]
    scaled = jnp.sqrt(delta_x * delta_x + delta_y * delta_y + delta_z * delta_z) / support_radius
    remain = jnp.maximum(1.0 - scaled, 0.0)
    return (remain ** 4 * (4.0 * scaled + 1.0)).astype(jnp.bfloat16)

def reference(sensitivity, node_xyz, ctrl_xyz, inverse):
    nodes_all = node_xyz.shape[1]
    span_rows = min(1024, nodes_all)
    steps_count = nodes_all // span_rows

    def advance(running, number):
        offset = (number * span_rows).astype(jnp.int32)
        node_part = lax.dynamic_slice_in_dim(node_xyz, offset, span_rows, 1)
        sens_part = lax.dynamic_slice_in_dim(sensitivity, offset, span_rows, 1)
        weights_tile = kernel_tile(node_part, ctrl_xyz)
        return (running + jnp.dot(sens_part, weights_tile, preferred_element_type=jnp.float32), None)
    start_sum = jnp.zeros((sensitivity.shape[0], ctrl_xyz.shape[1]), jnp.float32)
    pulled, _ = lax.scan(advance, start_sum, jnp.arange(steps_count, dtype=jnp.int32))
    pulled_low = pulled.astype(jnp.bfloat16)
    return jnp.dot(pulled_low, inverse, preferred_element_type=jnp.float32)
```

```python
import functools

import jax
import jax.numpy as jnp
from jax import lax
from jax.experimental import pallas as pl
from jax.experimental.pallas import tpu as pltpu
from jax.sharding import PartitionSpec as P

support_radius = 0.12
feature_rows = 32


def split_three(value):
    high = value.astype(jnp.bfloat16).astype(jnp.float32)
    rest = value - high
    middle = rest.astype(jnp.bfloat16).astype(jnp.float32)
    return high, middle, rest - middle


def feature_pair(xyz, is_node):
    ones = jnp.ones_like(xyz[0:1])
    rows = []
    scaled = (xyz - 0.5) * (4.0 / support_radius)
    for axis in range(3):
        high, middle, low = split_three(scaled[axis : axis + 1])
        if is_node:
            rows += [high, high, middle, middle, high, low]
        else:
            rows += [-2.0 * part for part in (high, middle, high, middle, low, high)]
    square = scaled * scaled
    total = square[0:1] + square[1:2] + square[2:3]
    parts = list(split_three(total))
    rows += parts + [ones] * 3 if is_node else [ones] * 3 + parts
    rows += [jnp.zeros_like(ones)] * (feature_rows - len(rows))
    return rows


def fill_features(wide_ref, xyz_ref, is_node):
    for index, row in enumerate(feature_pair(xyz_ref[...], is_node)):
        wide_ref[pl.ds(index, 1), :] = row


def weights_of(square):
    square = jnp.maximum(square, 1e-12)
    remain = jnp.maximum(4.0 - square * lax.rsqrt(square), 0.0)
    twice = remain * remain
    return ((twice * twice) * (5.0 - remain)).astype(jnp.bfloat16)


def pull_kernel(rows, span, block, sens_ref, node_ref, ctrl_ref, out_ref, node_wide, ctrl_wide, node_feat, ctrl_feat, sens_t):
    nodes, ctrls = node_ref.shape[1], ctrl_ref.shape[1]
    fill_features(node_wide, node_ref, True)
    fill_features(ctrl_wide, ctrl_ref, False)
    node_feat[...] = node_wide[...].astype(jnp.bfloat16)

    @pl.loop(0, nodes // block)
    def _(step):
        here = pl.ds(pl.multiple_of(step * block, block), block)
        sens_t[here, :] = sens_ref[:, here].astype(jnp.float32).T.astype(jnp.bfloat16)

    @pl.loop(0, ctrls // block)
    def _(step):
        here = pl.ds(pl.multiple_of(step * block, block), block)
        ctrl_feat[here, :] = ctrl_wide[:, here].T.astype(jnp.bfloat16)

    @pl.loop(0, ctrls // rows)
    def _(step):
        here = pl.ds(pl.multiple_of(step * rows, rows), rows)
        left = ctrl_feat[here, :]

        def advance(number, total):
            for part in range(span // block):
                offset = pl.multiple_of(number * span + part * block, block)
                square = jnp.dot(left, node_feat[:, pl.ds(offset, block)], preferred_element_type=jnp.float32)
                total = total + jnp.dot(weights_of(square), sens_t[pl.ds(offset, block), :], preferred_element_type=jnp.float32)
            return total

        total = lax.fori_loop(0, nodes // span, advance, jnp.zeros((rows, sens_t.shape[1]), jnp.float32))
        out_ref[:, here] = (total * (1.0 / 256.0)).T


def pull_part(sensitivity, node_xyz, ctrl_xyz):
    objs, nodes = sensitivity.shape
    ctrls = ctrl_xyz.shape[1]
    rows, span, block = min(512, ctrls), min(2048, nodes), min(256, nodes)
    return pl.pallas_call(
        functools.partial(pull_kernel, rows, span, block),
        out_shape=jax.ShapeDtypeStruct((objs, ctrls), jnp.float32),
        in_specs=[pl.BlockSpec(memory_space=pltpu.VMEM)] * 3,
        out_specs=pl.BlockSpec(memory_space=pltpu.VMEM),
        scratch_shapes=[
            pltpu.VMEM((feature_rows, nodes), jnp.float32),
            pltpu.VMEM((feature_rows, ctrls), jnp.float32),
            pltpu.VMEM((feature_rows, nodes), jnp.bfloat16),
            pltpu.VMEM((ctrls, feature_rows), jnp.bfloat16),
            pltpu.VMEM((nodes, objs), jnp.bfloat16),
        ],
        compiler_params=pltpu.CompilerParams(vmem_limit_bytes=48 * 2**20),
    )(sensitivity, node_xyz, ctrl_xyz)


def per_device(sensitivity, node_xyz, ctrl_xyz, inverse):
    partial_pull = pull_part(sensitivity, node_xyz, ctrl_xyz)
    pulled = lax.psum_scatter(partial_pull, "node", scatter_dimension=1, tiled=True)
    pulled_low = lax.all_gather(pulled.astype(jnp.bfloat16), "node", axis=1, tiled=True)
    product = jnp.dot(pulled_low, inverse, preferred_element_type=jnp.float32)
    return lax.psum_scatter(product, "ctrl", scatter_dimension=1, tiled=True)


def solution(mesh):
    in_specs = (P(None, "node"), P(None, "node"), P(None, "ctrl"), P("ctrl", "node"))
    out_specs = P(None, ("node", "ctrl"))
    return jax.shard_map(
        per_device, mesh=mesh, in_specs=in_specs, out_specs=out_specs, check_vma=False
    )
```

```python
import functools

import jax
import jax.numpy as jnp
from jax import lax
from jax.experimental import pallas as pl
from jax.experimental.pallas import tpu as pltpu
from jax.sharding import PartitionSpec as P

support_radius = 0.12
feature_rows = 32
max_chunks = 8


def split_three(value):
    high = value.astype(jnp.bfloat16).astype(jnp.float32)
    rest = value - high
    middle = rest.astype(jnp.bfloat16).astype(jnp.float32)
    return high, middle, rest - middle


def feature_pair(xyz, is_node):
    ones = jnp.ones_like(xyz[0:1])
    rows = []
    scaled = (xyz - 0.5) * (4.0 / support_radius)
    for axis in range(3):
        high, middle, low = split_three(scaled[axis : axis + 1])
        if is_node:
            rows += [high, high, middle, middle, high, low]
        else:
            rows += [-2.0 * part for part in (high, middle, high, middle, low, high)]
    square = scaled * scaled
    total = square[0:1] + square[1:2] + square[2:3]
    parts = list(split_three(total))
    rows += parts + [ones] * 3 if is_node else [ones] * 3 + parts
    rows += [jnp.zeros_like(ones)] * (feature_rows - len(rows))
    return rows


def fill_features(wide_ref, xyz_ref, is_node):
    for index, row in enumerate(feature_pair(xyz_ref[...], is_node)):
        wide_ref[pl.ds(index, 1), :] = row


def weights_of(square):
    square = jnp.maximum(square, 1e-12)
    remain = jnp.maximum(4.0 - square * lax.rsqrt(square), 0.0)
    twice = remain * remain
    return ((twice * twice) * (5.0 - remain)).astype(jnp.bfloat16)


def level_sizes(count):
    sizes = []
    while count % 2 == 0 and len(sizes) < 2:
        sizes.append(2)
        count //= 2
    return sizes + [count] if count > 1 else sizes


def fused_kernel(
    sizes, chunks, rows, span, block,
    sens_ref, node_ref, ctrl_ref, inverse_ref, out_ref,
    node_wide, ctrl_wide, node_feat, ctrl_feat, sens_t,
    inverse_here, inverse_sem, gathered, product, product_t, final, final_send, final_recv, *levels,
):
    nodes, ctrls = node_ref.shape[1], ctrl_ref.shape[1]
    depth = len(sizes)
    chunk = ctrls // chunks
    me = lax.axis_index("node")
    my_ctrl = lax.axis_index("ctrl")
    ctrl_count = final.shape[0] + 1
    own, sent, landed, rs_send, rs_recv, ag_send, ag_recv = [levels[i * depth : (i + 1) * depth] for i in range(7)]

    strides, lengths, coords, offsets = [], [chunk], [], [jnp.int32(0)]
    stride = 1
    for size in sizes:
        coord = lax.rem(lax.div(me, stride), size)
        strides.append(stride)
        lengths.append(lengths[-1] // size)
        coords.append(coord)
        offsets.append(offsets[-1] + coord * lengths[-1])
        stride *= size

    def peer_at(level, coord):
        return me + (coord - coords[level]) * strides[level]

    def around(level, turn):
        return lax.rem(coords[level] + turn + sizes[level], sizes[level])

    barrier = pltpu.get_barrier_semaphore()
    for level, size in enumerate(sizes):
        for turn in range(1, size):
            pl.semaphore_signal(barrier, inc=1, device_id={"node": peer_at(level, around(level, turn))}, device_id_type=pl.DeviceIdType.MESH)
    for turn in range(1, ctrl_count):
        other = lax.rem(my_ctrl + turn, ctrl_count)
        pl.semaphore_signal(barrier, inc=1, device_id={"ctrl": other}, device_id_type=pl.DeviceIdType.MESH)

    def inverse_copy(number):
        part = pl.ds(pl.multiple_of(number * chunk, chunk), chunk)
        return pltpu.make_async_copy(inverse_ref.at[part, :], inverse_here.at[part, :], inverse_sem.at[number])

    for number in range(chunks):
        inverse_copy(number).start()

    fill_features(node_wide, node_ref, True)
    fill_features(ctrl_wide, ctrl_ref, False)
    node_feat[...] = node_wide[...].astype(jnp.bfloat16)

    @pl.loop(0, nodes // block)
    def _(step):
        here = pl.ds(pl.multiple_of(step * block, block), block)
        sens_t[here, :] = sens_ref[:, here].astype(jnp.float32).T.astype(jnp.bfloat16)

    @pl.loop(0, ctrls // block)
    def _(step):
        here = pl.ds(pl.multiple_of(step * block, block), block)
        ctrl_feat[here, :] = ctrl_wide[:, here].T.astype(jnp.bfloat16)

    product[...] = jnp.zeros_like(product)
    pl.semaphore_wait(barrier, sum(size - 1 for size in sizes) + ctrl_count - 1)

    def scatter_copy(level, number, turn):
        coord = around(level, turn)
        length = lengths[level + 1]
        part = pl.ds(pl.multiple_of(coord * length, length), length)
        return pltpu.make_async_remote_copy(
            src_ref=sent[level].at[number, part, :],
            dst_ref=landed[level].at[number, turn - 1],
            send_sem=rs_send[level].at[number, turn - 1],
            recv_sem=rs_recv[level].at[number, turn - 1],
            device_id={"node": peer_at(level, coord)},
            device_id_type=pl.DeviceIdType.MESH,
        )

    def gather_copy(level, number, turn, arriving):
        length = lengths[level + 1]
        coord = around(level, -turn) if arriving else coords[level]
        start = offsets[level] + coord * length
        part = pl.ds(pl.multiple_of(start, length), length)
        return pltpu.make_async_remote_copy(
            src_ref=gathered.at[number, part, :],
            dst_ref=gathered.at[number, part, :],
            send_sem=ag_send[level].at[number, turn - 1],
            recv_sem=ag_recv[level].at[number, turn - 1],
            device_id={"node": peer_at(level, around(level, turn))},
            device_id_type=pl.DeviceIdType.MESH,
        )

    def start_scatter(level, number):
        for turn in range(1, sizes[level]):
            scatter_copy(level, number, turn).start()

    def start_gather(level, number):
        for turn in range(1, sizes[level]):
            gather_copy(level, number, turn, False).start()

    def compute(number):
        @pl.loop(0, chunk // rows)
        def _(step):
            there = pl.ds(pl.multiple_of(step * rows, rows), rows)
            left = ctrl_feat[pl.ds(pl.multiple_of(number * chunk + step * rows, rows), rows), :]

            def advance(index, total):
                for part in range(span // block):
                    offset = pl.multiple_of(index * span + part * block, block)
                    square = jnp.dot(left, node_feat[:, pl.ds(offset, block)], preferred_element_type=jnp.float32)
                    total = total + jnp.dot(weights_of(square), sens_t[pl.ds(offset, block), :], preferred_element_type=jnp.float32)
                return total

            own[0][number, there, :] = lax.fori_loop(0, nodes // span, advance, jnp.zeros((rows, sens_t.shape[1]), jnp.float32))

        start_scatter(0, number)

    def scatter_stage(level, number):
        length = lengths[level + 1]
        total = own[level][number, pl.ds(pl.multiple_of(coords[level] * length, length), length), :]
        for turn in range(1, sizes[level]):
            scatter_copy(level, number, turn).wait_recv()
            total = total + landed[level][number, turn - 1].astype(jnp.float32)
        if level + 1 < depth:
            own[level + 1][number] = total
            sent[level + 1][number] = total.astype(jnp.bfloat16)
            start_scatter(level + 1, number)
        else:
            part = pl.ds(pl.multiple_of(offsets[depth], length), length)
            gathered[number, part, :] = (total * (1.0 / 256.0)).astype(jnp.bfloat16)
            start_gather(level, number)

    def gather_stage(level, number):
        for turn in range(1, sizes[level]):
            gather_copy(level, number, turn, True).wait_recv()
        if level > 0:
            start_gather(level - 1, number)
        else:
            inverse_copy(number).wait()
            left = gathered[number].astype(jnp.float32).T.astype(jnp.bfloat16)
            part = pl.ds(pl.multiple_of(number * chunk, chunk), chunk)
            product[...] += jnp.dot(left, inverse_here[part, :], preferred_element_type=jnp.float32)

    stages = [compute]
    stages += [functools.partial(scatter_stage, level) for level in range(depth)]
    stages += [functools.partial(gather_stage, level) for level in reversed(range(depth))]

    @pl.loop(0, chunks + len(stages) - 1)
    def _(slot):
        for lag, stage in enumerate(stages):
            number = slot - lag

            @pl.when((number >= 0) & (number < chunks))
            def _():
                stage(number)

    width = final.shape[1]
    product_t[...] = product[...].T

    def final_copy(turn):
        other = lax.rem(my_ctrl + turn, ctrl_count)
        return pltpu.make_async_remote_copy(
            src_ref=product_t.at[pl.ds(pl.multiple_of(other * width, width), width), :],
            dst_ref=final.at[turn - 1],
            send_sem=final_send.at[turn - 1],
            recv_sem=final_recv.at[turn - 1],
            device_id={"ctrl": other},
            device_id_type=pl.DeviceIdType.MESH,
        )

    for turn in range(1, ctrl_count):
        final_copy(turn).start()

    @pl.loop(0, chunks)
    def _(number):
        for level, size in enumerate(sizes):
            for turn in range(1, size):
                scatter_copy(level, number, turn).wait_send()
                gather_copy(level, number, turn, False).wait_send()

    total = product_t[pl.ds(pl.multiple_of(my_ctrl * width, width), width), :]
    for turn in range(1, ctrl_count):
        final_copy(turn).wait_recv()
        total = total + final[turn - 1]
    out_ref[...] = total.T
    for turn in range(1, ctrl_count):
        final_copy(turn).wait_send()


def per_device(node_count, ctrl_count, sensitivity, node_xyz, ctrl_xyz, inverse):
    objs, nodes = sensitivity.shape
    ctrls, columns = inverse.shape
    sizes = level_sizes(node_count)
    chunks = max(1, min(max_chunks, ctrls // (16 * node_count)))
    chunk = ctrls // chunks
    rows, span, block = min(512, chunk), min(2048, nodes), min(256, nodes)
    lengths = [chunk]
    for size in sizes:
        lengths.append(lengths[-1] // size)
    depth = len(sizes)
    own = [pltpu.VMEM((chunks, lengths[level], objs), jnp.float32) for level in range(depth)]
    sent_types = [jnp.float32] + [jnp.bfloat16] * (depth - 1)
    sent = [pltpu.VMEM((chunks, lengths[level], objs), jnp.bfloat16) for level in range(1, depth)]
    landed = [pltpu.VMEM((chunks, sizes[level] - 1, lengths[level + 1], objs), sent_types[level]) for level in range(depth)]
    sems = [pltpu.SemaphoreType.DMA((chunks, size - 1)) for size in sizes]

    def kernel(*refs):
        first = len(refs) - (3 * depth - 1 + 4 * depth)
        levels = list(refs[first:])
        levels.insert(depth, levels[0])
        fused_kernel(sizes, chunks, rows, span, block, *refs[:first], *levels)

    width = columns // ctrl_count
    return pl.pallas_call(
        kernel,
        out_shape=jax.ShapeDtypeStruct((objs, width), jnp.float32),
        in_specs=[pl.BlockSpec(memory_space=pltpu.VMEM)] * 3 + [pl.BlockSpec(memory_space=pl.ANY)],
        out_specs=pl.BlockSpec(memory_space=pltpu.VMEM),
        scratch_shapes=[
            pltpu.VMEM((feature_rows, nodes), jnp.float32),
            pltpu.VMEM((feature_rows, ctrls), jnp.float32),
            pltpu.VMEM((feature_rows, nodes), jnp.bfloat16),
            pltpu.VMEM((ctrls, feature_rows), jnp.bfloat16),
            pltpu.VMEM((nodes, objs), jnp.bfloat16),
            pltpu.VMEM((ctrls, columns), jnp.bfloat16),
            pltpu.SemaphoreType.DMA((chunks,)),
            pltpu.VMEM((chunks, chunk, objs), jnp.bfloat16),
            pltpu.VMEM((objs, columns), jnp.float32),
            pltpu.VMEM((columns, objs), jnp.float32),
            pltpu.VMEM((ctrl_count - 1, width, objs), jnp.float32),
            pltpu.SemaphoreType.DMA((ctrl_count - 1,)),
            pltpu.SemaphoreType.DMA((ctrl_count - 1,)),
        ]
        + own + sent + landed + sems * 4,
        compiler_params=pltpu.CompilerParams(
            vmem_limit_bytes=56 * 2**20, collective_id=0, has_side_effects=True
        ),
    )(sensitivity, node_xyz, ctrl_xyz, inverse)


def solution(mesh):
    in_specs = (P(None, "node"), P(None, "node"), P(None, "ctrl"), P("ctrl", "node"))
    out_specs = P(None, ("node", "ctrl"))
    run = functools.partial(per_device, mesh.shape["node"], mesh.shape["ctrl"])
    return jax.shard_map(run, mesh=mesh, in_specs=in_specs, out_specs=out_specs, check_vma=False)
```

```python
import functools

import jax
import jax.numpy as jnp
from jax import lax
from jax.experimental import pallas as pl
from jax.experimental.pallas import tpu as pltpu
from jax.sharding import PartitionSpec as P

support_radius = 0.12
feature_rows = 32
max_chunks = 8


def split_three(value):
    high = value.astype(jnp.bfloat16).astype(jnp.float32)
    rest = value - high
    middle = rest.astype(jnp.bfloat16).astype(jnp.float32)
    return high, middle, rest - middle


def feature_pair(xyz, is_node):
    ones = jnp.ones_like(xyz[0:1])
    rows = []
    scaled = (xyz - 0.5) * (4.0 / support_radius)
    for axis in range(3):
        high, middle, low = split_three(scaled[axis : axis + 1])
        if is_node:
            rows += [high, high, middle, middle, high, low]
        else:
            rows += [-2.0 * part for part in (high, middle, high, middle, low, high)]
    square = scaled * scaled
    total = square[0:1] + square[1:2] + square[2:3]
    parts = list(split_three(total))
    rows += parts + [ones] * 3 if is_node else [ones] * 3 + parts
    rows += [jnp.zeros_like(ones)] * (feature_rows - len(rows))
    return rows


def fill_features(wide_ref, xyz_ref, is_node):
    for index, row in enumerate(feature_pair(xyz_ref[...], is_node)):
        wide_ref[pl.ds(index, 1), :] = row


def weights_of(square):
    square = jnp.maximum(square, 1e-12)
    remain = jnp.maximum(4.0 - square * lax.rsqrt(square), 0.0)
    twice = remain * remain
    return ((twice * twice) * (5.0 - remain)).astype(jnp.bfloat16)


def level_sizes(count):
    return [2, count // 2] if count % 2 == 0 and count > 2 else [count]


def fused_kernel(
    sizes, chunks, rows, span, block,
    sens_ref, node_ref, ctrl_ref, inverse_ref, out_ref,
    node_wide, ctrl_wide, node_feat, ctrl_feat,
    inverse_here, inverse_sem, gathered, product, product_t, final, final_send, final_recv, *levels,
):
    nodes, ctrls = node_ref.shape[1], ctrl_ref.shape[1]
    depth = len(sizes)
    chunk = ctrls // chunks
    me = lax.axis_index("node")
    my_ctrl = lax.axis_index("ctrl")
    ctrl_count = final.shape[0] + 1
    own, sent, landed, rs_send, rs_recv, ag_send, ag_recv = [levels[i * depth : (i + 1) * depth] for i in range(7)]

    strides, lengths, coords, offsets = [], [chunk], [], [jnp.int32(0)]
    stride = 1
    for size in sizes:
        coord = lax.rem(lax.div(me, stride), size)
        strides.append(stride)
        lengths.append(lengths[-1] // size)
        coords.append(coord)
        offsets.append(offsets[-1] + coord * lengths[-1])
        stride *= size

    def peer_at(level, coord):
        return me + (coord - coords[level]) * strides[level]

    def around(level, turn):
        return lax.rem(coords[level] + turn + sizes[level], sizes[level])

    barrier = pltpu.get_barrier_semaphore()
    for level, size in enumerate(sizes):
        for turn in range(1, size):
            pl.semaphore_signal(barrier, inc=1, device_id={"node": peer_at(level, around(level, turn))}, device_id_type=pl.DeviceIdType.MESH)
    for turn in range(1, ctrl_count):
        other = lax.rem(my_ctrl + turn, ctrl_count)
        pl.semaphore_signal(barrier, inc=1, device_id={"ctrl": other}, device_id_type=pl.DeviceIdType.MESH)

    def inverse_copy(number):
        part = pl.ds(pl.multiple_of(number * chunk, chunk), chunk)
        return pltpu.make_async_copy(inverse_ref.at[part, :], inverse_here.at[part, :], inverse_sem.at[number])

    for number in range(chunks):
        inverse_copy(number).start()

    fill_features(node_wide, node_ref, True)
    fill_features(ctrl_wide, ctrl_ref, False)
    ctrl_feat[...] = ctrl_wide[...].astype(jnp.bfloat16)

    @pl.loop(0, nodes // block)
    def _(step):
        here = pl.ds(pl.multiple_of(step * block, block), block)
        node_feat[here, :] = node_wide[:, here].T.astype(jnp.bfloat16)

    product[...] = jnp.zeros_like(product)
    pl.semaphore_wait(barrier, sum(size - 1 for size in sizes) + ctrl_count - 1)

    def scatter_copy(level, number, turn):
        coord = around(level, turn)
        length = lengths[level + 1]
        part = pl.ds(pl.multiple_of(coord * length, length), length)
        return pltpu.make_async_remote_copy(
            src_ref=sent[level].at[number, part, :],
            dst_ref=landed[level].at[number, turn - 1],
            send_sem=rs_send[level].at[number, turn - 1],
            recv_sem=rs_recv[level].at[number, turn - 1],
            device_id={"node": peer_at(level, coord)},
            device_id_type=pl.DeviceIdType.MESH,
        )

    def gather_copy(level, number, turn, arriving):
        length = lengths[level + 1]
        coord = around(level, -turn) if arriving else coords[level]
        start = offsets[level] + coord * length
        part = pl.ds(pl.multiple_of(start, length), length)
        return pltpu.make_async_remote_copy(
            src_ref=gathered.at[number, part, :],
            dst_ref=gathered.at[number, part, :],
            send_sem=ag_send[level].at[number, turn - 1],
            recv_sem=ag_recv[level].at[number, turn - 1],
            device_id={"node": peer_at(level, around(level, turn))},
            device_id_type=pl.DeviceIdType.MESH,
        )

    def start_scatter(level, number):
        for turn in range(1, sizes[level]):
            scatter_copy(level, number, turn).start()

    def start_gather(level, number):
        for turn in range(1, sizes[level]):
            gather_copy(level, number, turn, False).start()

    def compute(number):
        @pl.loop(0, chunk // rows)
        def _(step):
            there = pl.ds(pl.multiple_of(step * rows, rows), rows)
            right = ctrl_feat[:, pl.ds(pl.multiple_of(number * chunk + step * rows, rows), rows)]

            def advance(index, total):
                for part in range(span // block):
                    offset = pl.multiple_of(index * span + part * block, block)
                    square = jnp.dot(node_feat[pl.ds(offset, block), :], right, preferred_element_type=jnp.float32)
                    total = total + jnp.dot(sens_ref[:, pl.ds(offset, block)], weights_of(square), preferred_element_type=jnp.float32)
                return total

            own[0][number, there, :] = lax.fori_loop(0, nodes // span, advance, jnp.zeros((sens_ref.shape[0], rows), jnp.float32)).T

        start_scatter(0, number)

    def scatter_stage(level, number):
        length = lengths[level + 1]
        total = own[level][number, pl.ds(pl.multiple_of(coords[level] * length, length), length), :]
        for turn in range(1, sizes[level]):
            scatter_copy(level, number, turn).wait_recv()
            total = total + landed[level][number, turn - 1].astype(jnp.float32)
        if level + 1 < depth:
            own[level + 1][number] = total
            sent[level + 1][number] = total.astype(jnp.bfloat16)
            start_scatter(level + 1, number)
        else:
            part = pl.ds(pl.multiple_of(offsets[depth], length), length)
            gathered[number, part, :] = (total * (1.0 / 256.0)).astype(jnp.bfloat16)
            start_gather(level, number)

    def gather_stage(level, number):
        for turn in range(1, sizes[level]):
            gather_copy(level, number, turn, True).wait_recv()
        if level > 0:
            start_gather(level - 1, number)
        else:
            inverse_copy(number).wait()
            left = gathered[number].astype(jnp.float32).T.astype(jnp.bfloat16)
            part = pl.ds(pl.multiple_of(number * chunk, chunk), chunk)
            product[...] += jnp.dot(left, inverse_here[part, :], preferred_element_type=jnp.float32)

    stages = [compute]
    stages += [functools.partial(scatter_stage, level) for level in range(depth)]
    stages += [functools.partial(gather_stage, level) for level in reversed(range(depth))]

    @pl.loop(0, chunks + len(stages) - 1)
    def _(slot):
        for lag, stage in enumerate(stages):
            number = slot - lag

            @pl.when((number >= 0) & (number < chunks))
            def _():
                stage(number)

    width = final.shape[1]
    product_t[...] = product[...].T

    def final_copy(turn):
        other = lax.rem(my_ctrl + turn, ctrl_count)
        return pltpu.make_async_remote_copy(
            src_ref=product_t.at[pl.ds(pl.multiple_of(other * width, width), width), :],
            dst_ref=final.at[turn - 1],
            send_sem=final_send.at[turn - 1],
            recv_sem=final_recv.at[turn - 1],
            device_id={"ctrl": other},
            device_id_type=pl.DeviceIdType.MESH,
        )

    for turn in range(1, ctrl_count):
        final_copy(turn).start()

    @pl.loop(0, chunks)
    def _(number):
        for level, size in enumerate(sizes):
            for turn in range(1, size):
                scatter_copy(level, number, turn).wait_send()
                gather_copy(level, number, turn, False).wait_send()

    total = product_t[pl.ds(pl.multiple_of(my_ctrl * width, width), width), :]
    for turn in range(1, ctrl_count):
        final_copy(turn).wait_recv()
        total = total + final[turn - 1]
    out_ref[...] = total.T
    for turn in range(1, ctrl_count):
        final_copy(turn).wait_send()


def per_device(node_count, ctrl_count, sensitivity, node_xyz, ctrl_xyz, inverse):
    objs, nodes = sensitivity.shape
    ctrls, columns = inverse.shape
    sizes = level_sizes(node_count)
    chunks = max(1, min(max_chunks, ctrls // (16 * node_count)))
    chunk = ctrls // chunks
    rows, span, block = min(512, chunk), min(2048, nodes), min(256, nodes)
    lengths = [chunk]
    for size in sizes:
        lengths.append(lengths[-1] // size)
    depth = len(sizes)
    own = [pltpu.VMEM((chunks, lengths[level], objs), jnp.float32) for level in range(depth)]
    sent_types = [jnp.float32] + [jnp.bfloat16] * (depth - 1)
    sent = [pltpu.VMEM((chunks, lengths[level], objs), jnp.bfloat16) for level in range(1, depth)]
    landed = [pltpu.VMEM((chunks, sizes[level] - 1, lengths[level + 1], objs), sent_types[level]) for level in range(depth)]
    sems = [pltpu.SemaphoreType.DMA((chunks, size - 1)) for size in sizes]

    def kernel(*refs):
        first = len(refs) - (3 * depth - 1 + 4 * depth)
        levels = list(refs[first:])
        levels.insert(depth, levels[0])
        fused_kernel(sizes, chunks, rows, span, block, *refs[:first], *levels)

    width = columns // ctrl_count
    return pl.pallas_call(
        kernel,
        out_shape=jax.ShapeDtypeStruct((objs, width), jnp.float32),
        in_specs=[pl.BlockSpec(memory_space=pltpu.VMEM)] * 3 + [pl.BlockSpec(memory_space=pl.ANY)],
        out_specs=pl.BlockSpec(memory_space=pltpu.VMEM),
        scratch_shapes=[
            pltpu.VMEM((feature_rows, nodes), jnp.float32),
            pltpu.VMEM((feature_rows, ctrls), jnp.float32),
            pltpu.VMEM((nodes, feature_rows), jnp.bfloat16),
            pltpu.VMEM((feature_rows, ctrls), jnp.bfloat16),
            pltpu.VMEM((ctrls, columns), jnp.bfloat16),
            pltpu.SemaphoreType.DMA((chunks,)),
            pltpu.VMEM((chunks, chunk, objs), jnp.bfloat16),
            pltpu.VMEM((objs, columns), jnp.float32),
            pltpu.VMEM((columns, objs), jnp.float32),
            pltpu.VMEM((ctrl_count - 1, width, objs), jnp.float32),
            pltpu.SemaphoreType.DMA((ctrl_count - 1,)),
            pltpu.SemaphoreType.DMA((ctrl_count - 1,)),
        ]
        + own + sent + landed + sems * 4,
        compiler_params=pltpu.CompilerParams(
            vmem_limit_bytes=56 * 2**20, collective_id=0, has_side_effects=True
        ),
    )(sensitivity, node_xyz, ctrl_xyz, inverse)


def solution(mesh):
    in_specs = (P(None, "node"), P(None, "node"), P(None, "ctrl"), P("ctrl", "node"))
    out_specs = P(None, ("node", "ctrl"))
    run = functools.partial(per_device, mesh.shape["node"], mesh.shape["ctrl"])
    return jax.shard_map(run, mesh=mesh, in_specs=in_specs, out_specs=out_specs, check_vma=False)
```

```python
import functools

import jax
import jax.numpy as jnp
from jax import lax
from jax.experimental import pallas as pl
from jax.experimental.pallas import tpu as pltpu
from jax.sharding import PartitionSpec as P

support_radius = 0.12
feature_rows = 32
max_chunks = 8


def split_three(value):
    high = value.astype(jnp.bfloat16).astype(jnp.float32)
    rest = value - high
    middle = rest.astype(jnp.bfloat16).astype(jnp.float32)
    return high, middle, rest - middle


def feature_pair(xyz, is_node):
    ones = jnp.ones_like(xyz[0:1])
    rows = []
    scaled = (xyz - 0.5) * (4.0 / support_radius)
    for axis in range(3):
        high, middle, low = split_three(scaled[axis : axis + 1])
        if is_node:
            rows += [high, high, middle, middle, high, low]
        else:
            rows += [-2.0 * part for part in (high, middle, high, middle, low, high)]
    square = scaled * scaled
    total = square[0:1] + square[1:2] + square[2:3]
    parts = list(split_three(total))
    rows += parts + [ones] * 3 if is_node else [ones] * 3 + parts
    rows += [jnp.zeros_like(ones)] * (feature_rows - len(rows))
    return rows


def fill_features(wide_ref, xyz_ref, is_node):
    for index, row in enumerate(feature_pair(xyz_ref[...], is_node)):
        wide_ref[pl.ds(index, 1), :] = row


def weights_of(square):
    square = jnp.maximum(square, 1e-12)
    remain = jnp.maximum(4.0 - square * lax.rsqrt(square), 0.0)
    twice = remain * remain
    return ((twice * twice) * (5.0 - remain)).astype(jnp.bfloat16)


def level_sizes(count):
    return [2, count // 2] if count % 2 == 0 and count > 2 else [count]


def fused_kernel(
    sizes, chunks, rows, span, block,
    sens_ref, node_ref, ctrl_ref, inverse_ref, out_ref,
    node_wide, ctrl_wide, node_feat, ctrl_feat, sens_t,
    inverse_here, inverse_sem, gathered, product, product_t, product_low, final, final_send, final_recv, *levels,
):
    nodes, ctrls = node_ref.shape[1], ctrl_ref.shape[1]
    depth = len(sizes)
    chunk = ctrls // chunks
    me = lax.axis_index("node")
    my_ctrl = lax.axis_index("ctrl")
    ctrl_count = final.shape[0] + 1
    own, sent, landed, rs_send, rs_recv, ag_send, ag_recv = [levels[i * depth : (i + 1) * depth] for i in range(7)]

    strides, lengths, coords, offsets = [], [chunk], [], [jnp.int32(0)]
    stride = 1
    for size in sizes:
        coord = lax.rem(lax.div(me, stride), size)
        strides.append(stride)
        lengths.append(lengths[-1] // size)
        coords.append(coord)
        offsets.append(offsets[-1] + coord * lengths[-1])
        stride *= size

    def peer_at(level, coord):
        return me + (coord - coords[level]) * strides[level]

    def around(level, turn):
        return lax.rem(coords[level] + turn + sizes[level], sizes[level])

    barrier = pltpu.get_barrier_semaphore()
    for level, size in enumerate(sizes):
        for turn in range(1, size):
            pl.semaphore_signal(barrier, inc=1, device_id={"node": peer_at(level, around(level, turn))}, device_id_type=pl.DeviceIdType.MESH)
    for turn in range(1, ctrl_count):
        other = lax.rem(my_ctrl + turn, ctrl_count)
        pl.semaphore_signal(barrier, inc=1, device_id={"ctrl": other}, device_id_type=pl.DeviceIdType.MESH)

    def inverse_copy(number):
        part = pl.ds(pl.multiple_of(number * chunk, chunk), chunk)
        return pltpu.make_async_copy(inverse_ref.at[part, :], inverse_here.at[part, :], inverse_sem.at[number])

    for number in range(chunks):
        inverse_copy(number).start()

    fill_features(node_wide, node_ref, True)
    fill_features(ctrl_wide, ctrl_ref, False)
    node_feat[...] = node_wide[...].astype(jnp.bfloat16)

    @pl.loop(0, nodes // block)
    def _(step):
        here = pl.ds(pl.multiple_of(step * block, block), block)
        sens_t[here, :] = sens_ref[:, here].astype(jnp.float32).T.astype(jnp.bfloat16)

    @pl.loop(0, ctrls // block)
    def _(step):
        here = pl.ds(pl.multiple_of(step * block, block), block)
        ctrl_feat[here, :] = ctrl_wide[:, here].T.astype(jnp.bfloat16)

    product[...] = jnp.zeros_like(product)
    pl.semaphore_wait(barrier, sum(size - 1 for size in sizes) + ctrl_count - 1)

    def scatter_copy(level, number, turn):
        coord = around(level, turn)
        length = lengths[level + 1]
        part = pl.ds(pl.multiple_of(coord * length, length), length)
        return pltpu.make_async_remote_copy(
            src_ref=sent[level].at[number, part, :],
            dst_ref=landed[level].at[number, turn - 1],
            send_sem=rs_send[level].at[number, turn - 1],
            recv_sem=rs_recv[level].at[number, turn - 1],
            device_id={"node": peer_at(level, coord)},
            device_id_type=pl.DeviceIdType.MESH,
        )

    def gather_copy(level, number, turn, arriving):
        length = lengths[level + 1]
        coord = around(level, -turn) if arriving else coords[level]
        start = offsets[level] + coord * length
        part = pl.ds(pl.multiple_of(start, length), length)
        return pltpu.make_async_remote_copy(
            src_ref=gathered.at[number, part, :],
            dst_ref=gathered.at[number, part, :],
            send_sem=ag_send[level].at[number, turn - 1],
            recv_sem=ag_recv[level].at[number, turn - 1],
            device_id={"node": peer_at(level, around(level, turn))},
            device_id_type=pl.DeviceIdType.MESH,
        )

    def start_scatter(level, number):
        for turn in range(1, sizes[level]):
            scatter_copy(level, number, turn).start()

    def start_gather(level, number):
        for turn in range(1, sizes[level]):
            gather_copy(level, number, turn, False).start()

    def compute(number):
        @pl.loop(0, chunk // rows)
        def _(step):
            there = pl.ds(pl.multiple_of(step * rows, rows), rows)
            left = ctrl_feat[pl.ds(pl.multiple_of(number * chunk + step * rows, rows), rows), :]

            def advance(index, total):
                for part in range(span // block):
                    offset = pl.multiple_of(index * span + part * block, block)
                    square = jnp.dot(left, node_feat[:, pl.ds(offset, block)], preferred_element_type=jnp.float32)
                    total = total + jnp.dot(weights_of(square), sens_t[pl.ds(offset, block), :], preferred_element_type=jnp.float32)
                return total

            own[0][number, there, :] = lax.fori_loop(0, nodes // span, advance, jnp.zeros((rows, sens_t.shape[1]), jnp.float32))

        start_scatter(0, number)

    def scatter_stage(level, number):
        length = lengths[level + 1]
        total = own[level][number, pl.ds(pl.multiple_of(coords[level] * length, length), length), :]
        for turn in range(1, sizes[level]):
            scatter_copy(level, number, turn).wait_recv()
            total = total + landed[level][number, turn - 1].astype(jnp.float32)
        if level + 1 < depth:
            own[level + 1][number] = total
            sent[level + 1][number] = total.astype(jnp.bfloat16)
            start_scatter(level + 1, number)
        else:
            part = pl.ds(pl.multiple_of(offsets[depth], length), length)
            gathered[number, part, :] = (total * (1.0 / 256.0)).astype(jnp.bfloat16)
            start_gather(level, number)

    def gather_stage(level, number):
        for turn in range(1, sizes[level]):
            gather_copy(level, number, turn, True).wait_recv()
        if level > 0:
            start_gather(level - 1, number)
        else:
            inverse_copy(number).wait()
            left = gathered[number].astype(jnp.float32).T.astype(jnp.bfloat16)
            part = pl.ds(pl.multiple_of(number * chunk, chunk), chunk)
            product[...] += jnp.dot(left, inverse_here[part, :], preferred_element_type=jnp.float32)

    stages = [compute]
    stages += [functools.partial(scatter_stage, level) for level in range(depth)]
    stages += [functools.partial(gather_stage, level) for level in reversed(range(depth))]

    @pl.loop(0, chunks + len(stages) - 1)
    def _(slot):
        for lag, stage in enumerate(stages):
            number = slot - lag

            @pl.when((number >= 0) & (number < chunks))
            def _():
                stage(number)

    width = final.shape[1]
    product_t[...] = product[...].T
    product_low[...] = product_t[...].astype(jnp.bfloat16)

    def final_copy(turn):
        other = lax.rem(my_ctrl + turn, ctrl_count)
        return pltpu.make_async_remote_copy(
            src_ref=product_low.at[pl.ds(pl.multiple_of(other * width, width), width), :],
            dst_ref=final.at[turn - 1],
            send_sem=final_send.at[turn - 1],
            recv_sem=final_recv.at[turn - 1],
            device_id={"ctrl": other},
            device_id_type=pl.DeviceIdType.MESH,
        )

    for turn in range(1, ctrl_count):
        final_copy(turn).start()

    @pl.loop(0, chunks)
    def _(number):
        for level, size in enumerate(sizes):
            for turn in range(1, size):
                scatter_copy(level, number, turn).wait_send()
                gather_copy(level, number, turn, False).wait_send()

    total = product_t[pl.ds(pl.multiple_of(my_ctrl * width, width), width), :]
    for turn in range(1, ctrl_count):
        final_copy(turn).wait_recv()
        total = total + final[turn - 1].astype(jnp.float32)
    out_ref[...] = total.T
    for turn in range(1, ctrl_count):
        final_copy(turn).wait_send()


def per_device(node_count, ctrl_count, sensitivity, node_xyz, ctrl_xyz, inverse):
    objs, nodes = sensitivity.shape
    ctrls, columns = inverse.shape
    sizes = level_sizes(node_count)
    chunks = max(1, min(max_chunks, ctrls // (16 * node_count)))
    chunk = ctrls // chunks
    rows, span, block = min(1024, chunk), min(2048, nodes), min(256, nodes)
    lengths = [chunk]
    for size in sizes:
        lengths.append(lengths[-1] // size)
    depth = len(sizes)
    own = [pltpu.VMEM((chunks, lengths[level], objs), jnp.float32) for level in range(depth)]
    sent_types = [jnp.float32] + [jnp.bfloat16] * (depth - 1)
    sent = [pltpu.VMEM((chunks, lengths[level], objs), jnp.bfloat16) for level in range(1, depth)]
    landed = [pltpu.VMEM((chunks, sizes[level] - 1, lengths[level + 1], objs), sent_types[level]) for level in range(depth)]
    sems = [pltpu.SemaphoreType.DMA((chunks, size - 1)) for size in sizes]

    def kernel(*refs):
        first = len(refs) - (3 * depth - 1 + 4 * depth)
        levels = list(refs[first:])
        levels.insert(depth, levels[0])
        fused_kernel(sizes, chunks, rows, span, block, *refs[:first], *levels)

    width = columns // ctrl_count
    return pl.pallas_call(
        kernel,
        out_shape=jax.ShapeDtypeStruct((objs, width), jnp.float32),
        in_specs=[pl.BlockSpec(memory_space=pltpu.VMEM)] * 3 + [pl.BlockSpec(memory_space=pl.ANY)],
        out_specs=pl.BlockSpec(memory_space=pltpu.VMEM),
        scratch_shapes=[
            pltpu.VMEM((feature_rows, nodes), jnp.float32),
            pltpu.VMEM((feature_rows, ctrls), jnp.float32),
            pltpu.VMEM((feature_rows, nodes), jnp.bfloat16),
            pltpu.VMEM((ctrls, feature_rows), jnp.bfloat16),
            pltpu.VMEM((nodes, objs), jnp.bfloat16),
            pltpu.VMEM((ctrls, columns), jnp.bfloat16),
            pltpu.SemaphoreType.DMA((chunks,)),
            pltpu.VMEM((chunks, chunk, objs), jnp.bfloat16),
            pltpu.VMEM((objs, columns), jnp.float32),
            pltpu.VMEM((columns, objs), jnp.float32),
            pltpu.VMEM((columns, objs), jnp.bfloat16),
            pltpu.VMEM((ctrl_count - 1, width, objs), jnp.bfloat16),
            pltpu.SemaphoreType.DMA((ctrl_count - 1,)),
            pltpu.SemaphoreType.DMA((ctrl_count - 1,)),
        ]
        + own + sent + landed + sems * 4,
        compiler_params=pltpu.CompilerParams(
            vmem_limit_bytes=56 * 2**20, collective_id=0, has_side_effects=True
        ),
    )(sensitivity, node_xyz, ctrl_xyz, inverse)


def solution(mesh):
    in_specs = (P(None, "node"), P(None, "node"), P(None, "ctrl"), P("ctrl", "node"))
    out_specs = P(None, ("node", "ctrl"))
    run = functools.partial(per_device, mesh.shape["node"], mesh.shape["ctrl"])
    return jax.shard_map(run, mesh=mesh, in_specs=in_specs, out_specs=out_specs, check_vma=False)
```

```python
import functools

import jax
import jax.numpy as jnp
from jax import lax
from jax.experimental import pallas as pl
from jax.experimental.pallas import tpu as pltpu
from jax.sharding import PartitionSpec as P

support_radius = 0.12
feature_rows = 32
max_chunks = 8
half_per_log_two = 0.7213475204444817


def split_three(value):
    high = value.astype(jnp.bfloat16).astype(jnp.float32)
    rest = value - high
    middle = rest.astype(jnp.bfloat16).astype(jnp.float32)
    return high, middle, rest - middle


def feature_pair(xyz, is_node):
    ones = jnp.ones_like(xyz[0:1])
    rows = []
    scaled = (xyz - 0.5) * (4.0 / support_radius)
    for axis in range(3):
        high, middle, low = split_three(scaled[axis : axis + 1])
        if is_node:
            rows += [high, high, middle, middle, high, low]
        else:
            rows += [-2.0 * part for part in (high, middle, high, middle, low, high)]
    square = scaled * scaled
    total = square[0:1] + square[1:2] + square[2:3]
    parts = list(split_three(total))
    rows += parts + [ones] * 3 if is_node else [ones] * 3 + parts
    rows += [jnp.zeros_like(ones)] * (feature_rows - len(rows))
    return rows


def fill_features(wide_ref, xyz_ref, is_node):
    for index, row in enumerate(feature_pair(xyz_ref[...], is_node)):
        wide_ref[pl.ds(index, 1), :] = row


def weights_of(square):
    square = jnp.maximum(square, 1e-12)
    remain = jnp.maximum(4.0 - jnp.exp2(jnp.log(square) * half_per_log_two), 0.0)
    twice = remain * remain
    return ((twice * twice) * (5.0 - remain)).astype(jnp.bfloat16)


def level_sizes(count):
    return [2, count // 2] if count % 2 == 0 and count > 2 else [count]


def fused_kernel(
    sizes, chunks, rows, span, block,
    sens_ref, node_ref, ctrl_ref, inverse_ref, out_ref,
    node_wide, ctrl_wide, node_feat, ctrl_feat, sens_t,
    inverse_here, inverse_sem, gathered, product, product_t, product_low, final, final_send, final_recv, *levels,
):
    nodes, ctrls = node_ref.shape[1], ctrl_ref.shape[1]
    depth = len(sizes)
    chunk = ctrls // chunks
    me = lax.axis_index("node")
    my_ctrl = lax.axis_index("ctrl")
    ctrl_count = final.shape[0] + 1
    own, sent, landed, rs_send, rs_recv, ag_send, ag_recv = [levels[i * depth : (i + 1) * depth] for i in range(7)]

    strides, lengths, coords, offsets = [], [chunk], [], [jnp.int32(0)]
    stride = 1
    for size in sizes:
        coord = lax.rem(lax.div(me, stride), size)
        strides.append(stride)
        lengths.append(lengths[-1] // size)
        coords.append(coord)
        offsets.append(offsets[-1] + coord * lengths[-1])
        stride *= size

    def peer_at(level, coord):
        return me + (coord - coords[level]) * strides[level]

    def around(level, turn):
        return lax.rem(coords[level] + turn + sizes[level], sizes[level])

    barrier = pltpu.get_barrier_semaphore()
    for level, size in enumerate(sizes):
        for turn in range(1, size):
            pl.semaphore_signal(barrier, inc=1, device_id={"node": peer_at(level, around(level, turn))}, device_id_type=pl.DeviceIdType.MESH)
    for turn in range(1, ctrl_count):
        other = lax.rem(my_ctrl + turn, ctrl_count)
        pl.semaphore_signal(barrier, inc=1, device_id={"ctrl": other}, device_id_type=pl.DeviceIdType.MESH)

    def inverse_copy(number):
        part = pl.ds(pl.multiple_of(number * chunk, chunk), chunk)
        return pltpu.make_async_copy(inverse_ref.at[part, :], inverse_here.at[part, :], inverse_sem.at[number])

    for number in range(chunks):
        inverse_copy(number).start()

    fill_features(node_wide, node_ref, True)
    fill_features(ctrl_wide, ctrl_ref, False)
    node_feat[...] = node_wide[...].astype(jnp.bfloat16)

    @pl.loop(0, nodes // block)
    def _(step):
        here = pl.ds(pl.multiple_of(step * block, block), block)
        sens_t[here, :] = sens_ref[:, here].astype(jnp.float32).T.astype(jnp.bfloat16)

    @pl.loop(0, ctrls // block)
    def _(step):
        here = pl.ds(pl.multiple_of(step * block, block), block)
        ctrl_feat[here, :] = ctrl_wide[:, here].T.astype(jnp.bfloat16)

    product[...] = jnp.zeros_like(product)
    pl.semaphore_wait(barrier, sum(size - 1 for size in sizes) + ctrl_count - 1)

    def scatter_copy(level, number, turn):
        coord = around(level, turn)
        length = lengths[level + 1]
        part = pl.ds(pl.multiple_of(coord * length, length), length)
        return pltpu.make_async_remote_copy(
            src_ref=sent[level].at[number, part, :],
            dst_ref=landed[level].at[number, turn - 1],
            send_sem=rs_send[level].at[number, turn - 1],
            recv_sem=rs_recv[level].at[number, turn - 1],
            device_id={"node": peer_at(level, coord)},
            device_id_type=pl.DeviceIdType.MESH,
        )

    def gather_copy(level, number, turn, arriving):
        length = lengths[level + 1]
        coord = around(level, -turn) if arriving else coords[level]
        start = offsets[level] + coord * length
        part = pl.ds(pl.multiple_of(start, length), length)
        return pltpu.make_async_remote_copy(
            src_ref=gathered.at[number, part, :],
            dst_ref=gathered.at[number, part, :],
            send_sem=ag_send[level].at[number, turn - 1],
            recv_sem=ag_recv[level].at[number, turn - 1],
            device_id={"node": peer_at(level, around(level, turn))},
            device_id_type=pl.DeviceIdType.MESH,
        )

    def start_scatter(level, number):
        for turn in range(1, sizes[level]):
            scatter_copy(level, number, turn).start()

    def start_gather(level, number):
        for turn in range(1, sizes[level]):
            gather_copy(level, number, turn, False).start()

    def compute(number):
        @pl.loop(0, chunk // rows)
        def _(step):
            there = pl.ds(pl.multiple_of(step * rows, rows), rows)
            left = ctrl_feat[pl.ds(pl.multiple_of(number * chunk + step * rows, rows), rows), :]

            def advance(index, total):
                for part in range(span // block):
                    offset = pl.multiple_of(index * span + part * block, block)
                    square = jnp.dot(left, node_feat[:, pl.ds(offset, block)], preferred_element_type=jnp.float32)
                    total = total + jnp.dot(weights_of(square), sens_t[pl.ds(offset, block), :], preferred_element_type=jnp.float32)
                return total

            own[0][number, there, :] = lax.fori_loop(0, nodes // span, advance, jnp.zeros((rows, sens_t.shape[1]), jnp.float32))

        start_scatter(0, number)

    def scatter_stage(level, number):
        length = lengths[level + 1]
        total = own[level][number, pl.ds(pl.multiple_of(coords[level] * length, length), length), :]
        for turn in range(1, sizes[level]):
            scatter_copy(level, number, turn).wait_recv()
            total = total + landed[level][number, turn - 1].astype(jnp.float32)
        if level + 1 < depth:
            own[level + 1][number] = total
            sent[level + 1][number] = total.astype(jnp.bfloat16)
            start_scatter(level + 1, number)
        else:
            part = pl.ds(pl.multiple_of(offsets[depth], length), length)
            gathered[number, part, :] = (total * (1.0 / 256.0)).astype(jnp.bfloat16)
            start_gather(level, number)

    def gather_stage(level, number):
        for turn in range(1, sizes[level]):
            gather_copy(level, number, turn, True).wait_recv()
        if level > 0:
            start_gather(level - 1, number)
        else:
            inverse_copy(number).wait()
            left = gathered[number].astype(jnp.float32).T.astype(jnp.bfloat16)
            part = pl.ds(pl.multiple_of(number * chunk, chunk), chunk)
            product[...] += jnp.dot(left, inverse_here[part, :], preferred_element_type=jnp.float32)

    stages = [compute]
    stages += [functools.partial(scatter_stage, level) for level in range(depth)]
    stages += [functools.partial(gather_stage, level) for level in reversed(range(depth))]

    @pl.loop(0, chunks + len(stages) - 1)
    def _(slot):
        for lag, stage in enumerate(stages):
            number = slot - lag

            @pl.when((number >= 0) & (number < chunks))
            def _():
                stage(number)

    width = final.shape[1]
    product_t[...] = product[...].T
    product_low[...] = product_t[...].astype(jnp.bfloat16)

    def final_copy(turn):
        other = lax.rem(my_ctrl + turn, ctrl_count)
        return pltpu.make_async_remote_copy(
            src_ref=product_low.at[pl.ds(pl.multiple_of(other * width, width), width), :],
            dst_ref=final.at[turn - 1],
            send_sem=final_send.at[turn - 1],
            recv_sem=final_recv.at[turn - 1],
            device_id={"ctrl": other},
            device_id_type=pl.DeviceIdType.MESH,
        )

    for turn in range(1, ctrl_count):
        final_copy(turn).start()

    @pl.loop(0, chunks)
    def _(number):
        for level, size in enumerate(sizes):
            for turn in range(1, size):
                scatter_copy(level, number, turn).wait_send()
                gather_copy(level, number, turn, False).wait_send()

    total = product_t[pl.ds(pl.multiple_of(my_ctrl * width, width), width), :]
    for turn in range(1, ctrl_count):
        final_copy(turn).wait_recv()
        total = total + final[turn - 1].astype(jnp.float32)
    out_ref[...] = total.T
    for turn in range(1, ctrl_count):
        final_copy(turn).wait_send()


def per_device(node_count, ctrl_count, sensitivity, node_xyz, ctrl_xyz, inverse):
    objs, nodes = sensitivity.shape
    ctrls, columns = inverse.shape
    sizes = level_sizes(node_count)
    chunks = max(1, min(max_chunks, ctrls // (16 * node_count)))
    chunk = ctrls // chunks
    rows, span, block = min(1024, chunk), min(2048, nodes), min(256, nodes)
    lengths = [chunk]
    for size in sizes:
        lengths.append(lengths[-1] // size)
    depth = len(sizes)
    own = [pltpu.VMEM((chunks, lengths[level], objs), jnp.float32) for level in range(depth)]
    sent_types = [jnp.float32] + [jnp.bfloat16] * (depth - 1)
    sent = [pltpu.VMEM((chunks, lengths[level], objs), jnp.bfloat16) for level in range(1, depth)]
    landed = [pltpu.VMEM((chunks, sizes[level] - 1, lengths[level + 1], objs), sent_types[level]) for level in range(depth)]
    sems = [pltpu.SemaphoreType.DMA((chunks, size - 1)) for size in sizes]

    def kernel(*refs):
        first = len(refs) - (3 * depth - 1 + 4 * depth)
        levels = list(refs[first:])
        levels.insert(depth, levels[0])
        fused_kernel(sizes, chunks, rows, span, block, *refs[:first], *levels)

    width = columns // ctrl_count
    return pl.pallas_call(
        kernel,
        out_shape=jax.ShapeDtypeStruct((objs, width), jnp.float32),
        in_specs=[pl.BlockSpec(memory_space=pltpu.VMEM)] * 3 + [pl.BlockSpec(memory_space=pl.ANY)],
        out_specs=pl.BlockSpec(memory_space=pltpu.VMEM),
        scratch_shapes=[
            pltpu.VMEM((feature_rows, nodes), jnp.float32),
            pltpu.VMEM((feature_rows, ctrls), jnp.float32),
            pltpu.VMEM((feature_rows, nodes), jnp.bfloat16),
            pltpu.VMEM((ctrls, feature_rows), jnp.bfloat16),
            pltpu.VMEM((nodes, objs), jnp.bfloat16),
            pltpu.VMEM((ctrls, columns), jnp.bfloat16),
            pltpu.SemaphoreType.DMA((chunks,)),
            pltpu.VMEM((chunks, chunk, objs), jnp.bfloat16),
            pltpu.VMEM((objs, columns), jnp.float32),
            pltpu.VMEM((columns, objs), jnp.float32),
            pltpu.VMEM((columns, objs), jnp.bfloat16),
            pltpu.VMEM((ctrl_count - 1, width, objs), jnp.bfloat16),
            pltpu.SemaphoreType.DMA((ctrl_count - 1,)),
            pltpu.SemaphoreType.DMA((ctrl_count - 1,)),
        ]
        + own + sent + landed + sems * 4,
        compiler_params=pltpu.CompilerParams(
            vmem_limit_bytes=56 * 2**20, collective_id=0, has_side_effects=True
        ),
    )(sensitivity, node_xyz, ctrl_xyz, inverse)


def solution(mesh):
    in_specs = (P(None, "node"), P(None, "node"), P(None, "ctrl"), P("ctrl", "node"))
    out_specs = P(None, ("node", "ctrl"))
    run = functools.partial(per_device, mesh.shape["node"], mesh.shape["ctrl"])
    return jax.shard_map(run, mesh=mesh, in_specs=in_specs, out_specs=out_specs, check_vma=False)
```

```python
import functools

import jax
import jax.numpy as jnp
from jax import lax
from jax.experimental import pallas as pl
from jax.experimental.pallas import tpu as pltpu
from jax.sharding import PartitionSpec as P

support_radius = 0.12
feature_rows = 32
max_chunks = 8
ctrl_plain, node_plain = 24, 27
lanes = 128


def split_three(value):
    high = value.astype(jnp.bfloat16).astype(jnp.float32)
    rest = value - high
    middle = rest.astype(jnp.bfloat16).astype(jnp.float32)
    return high, middle, rest - middle


def feature_pair(xyz, is_node):
    ones = jnp.ones_like(xyz[0:1])
    rows = []
    scaled = (xyz - 0.5) * (4.0 / support_radius)
    for axis in range(3):
        high, middle, low = split_three(scaled[axis : axis + 1])
        if is_node:
            rows += [high, high, middle, middle, high, low]
        else:
            rows += [-2.0 * part for part in (high, middle, high, middle, low, high)]
    square = scaled * scaled
    total = square[0:1] + square[1:2] + square[2:3]
    parts = list(split_three(total))
    rows += parts + [ones] * 3 if is_node else [ones] * 3 + parts
    plain, zeros = [scaled[axis : axis + 1] for axis in range(3)], [jnp.zeros_like(ones)] * 3
    rows += zeros + plain if is_node else plain + zeros
    rows += [jnp.zeros_like(ones)] * (feature_rows - len(rows))
    return rows


def fill_features(wide_ref, xyz_ref, is_node):
    for index, row in enumerate(feature_pair(xyz_ref[...], is_node)):
        wide_ref[pl.ds(index, 1), :] = row


def weights_of(square):
    square = jnp.maximum(square, 1e-12)
    remain = jnp.maximum(4.0 - square * lax.rsqrt(square), 0.0)
    twice = remain * remain
    return ((twice * twice) * (5.0 - remain)).astype(jnp.bfloat16)


def level_sizes(count):
    return [2, count // 2] if count % 2 == 0 and count > 2 else [count]


def fused_kernel(
    sizes, chunks, rows, span, block,
    sens_ref, node_ref, ctrl_ref, inverse_ref, out_ref,
    node_wide, ctrl_wide, node_feat, ctrl_feat, sens_t, ctrl_spread,
    inverse_here, inverse_sem, gathered, product, product_t, product_low, final, final_send, final_recv, *levels,
):
    nodes, ctrls = node_ref.shape[1], ctrl_ref.shape[1]
    depth = len(sizes)
    chunk = ctrls // chunks
    me = lax.axis_index("node")
    my_ctrl = lax.axis_index("ctrl")
    ctrl_count = final.shape[0] + 1
    own, sent, landed, rs_send, rs_recv, ag_send, ag_recv = [levels[i * depth : (i + 1) * depth] for i in range(7)]

    strides, lengths, coords, offsets = [], [chunk], [], [jnp.int32(0)]
    stride = 1
    for size in sizes:
        coord = lax.rem(lax.div(me, stride), size)
        strides.append(stride)
        lengths.append(lengths[-1] // size)
        coords.append(coord)
        offsets.append(offsets[-1] + coord * lengths[-1])
        stride *= size

    def peer_at(level, coord):
        return me + (coord - coords[level]) * strides[level]

    def around(level, turn):
        return lax.rem(coords[level] + turn + sizes[level], sizes[level])

    barrier = pltpu.get_barrier_semaphore()
    for level, size in enumerate(sizes):
        for turn in range(1, size):
            pl.semaphore_signal(barrier, inc=1, device_id={"node": peer_at(level, around(level, turn))}, device_id_type=pl.DeviceIdType.MESH)
    for turn in range(1, ctrl_count):
        other = lax.rem(my_ctrl + turn, ctrl_count)
        pl.semaphore_signal(barrier, inc=1, device_id={"ctrl": other}, device_id_type=pl.DeviceIdType.MESH)

    def inverse_copy(number):
        part = pl.ds(pl.multiple_of(number * chunk, chunk), chunk)
        return pltpu.make_async_copy(inverse_ref.at[part, :], inverse_here.at[part, :], inverse_sem.at[number])

    for number in range(chunks):
        inverse_copy(number).start()

    fill_features(node_wide, node_ref, True)
    fill_features(ctrl_wide, ctrl_ref, False)
    node_feat[...] = node_wide[...].astype(jnp.bfloat16)

    @pl.loop(0, nodes // block)
    def _(step):
        here = pl.ds(pl.multiple_of(step * block, block), block)
        sens_t[here, :] = sens_ref[:, here].astype(jnp.float32).T.astype(jnp.bfloat16)

    @pl.loop(0, ctrls // block)
    def _(step):
        here = pl.ds(pl.multiple_of(step * block, block), block)
        turned = ctrl_wide[:, here].T
        ctrl_feat[here, :] = turned.astype(jnp.bfloat16)
        for axis in range(3):
            ctrl_spread[axis, here, :] = jnp.broadcast_to(turned[:, ctrl_plain + axis : ctrl_plain + axis + 1], (block, lanes))

    product[...] = jnp.zeros_like(product)
    pl.semaphore_wait(barrier, sum(size - 1 for size in sizes) + ctrl_count - 1)

    def scatter_copy(level, number, turn):
        coord = around(level, turn)
        length = lengths[level + 1]
        part = pl.ds(pl.multiple_of(coord * length, length), length)
        return pltpu.make_async_remote_copy(
            src_ref=sent[level].at[number, part, :],
            dst_ref=landed[level].at[number, turn - 1],
            send_sem=rs_send[level].at[number, turn - 1],
            recv_sem=rs_recv[level].at[number, turn - 1],
            device_id={"node": peer_at(level, coord)},
            device_id_type=pl.DeviceIdType.MESH,
        )

    def gather_copy(level, number, turn, arriving):
        length = lengths[level + 1]
        coord = around(level, -turn) if arriving else coords[level]
        start = offsets[level] + coord * length
        part = pl.ds(pl.multiple_of(start, length), length)
        return pltpu.make_async_remote_copy(
            src_ref=gathered.at[number, part, :],
            dst_ref=gathered.at[number, part, :],
            send_sem=ag_send[level].at[number, turn - 1],
            recv_sem=ag_recv[level].at[number, turn - 1],
            device_id={"node": peer_at(level, around(level, turn))},
            device_id_type=pl.DeviceIdType.MESH,
        )

    def start_scatter(level, number):
        for turn in range(1, sizes[level]):
            scatter_copy(level, number, turn).start()

    def start_gather(level, number):
        for turn in range(1, sizes[level]):
            gather_copy(level, number, turn, False).start()

    def plain_square(here, offset):
        total = None
        for axis in range(3):
            node_row = node_wide[pl.ds(node_plain + axis, 1), pl.ds(pl.multiple_of(offset, lanes), lanes)]
            delta = ctrl_spread[axis, here, :] - node_row
            total = delta * delta if total is None else total + delta * delta
        return total

    def compute(number):
        @pl.loop(0, chunk // rows)
        def _(step):
            there = pl.ds(pl.multiple_of(step * rows, rows), rows)
            here = pl.ds(pl.multiple_of(number * chunk + step * rows, rows), rows)
            left = ctrl_feat[here, :]

            def advance(index, total):
                for part in range(span // block):
                    offset = pl.multiple_of(index * span + part * block, block)
                    if part % 3 == 1 and block % lanes == 0:
                        weights = jnp.concatenate([weights_of(plain_square(here, offset + piece * lanes)) for piece in range(block // lanes)], axis=1)
                    else:
                        weights = weights_of(jnp.dot(left, node_feat[:, pl.ds(offset, block)], preferred_element_type=jnp.float32))
                    total = total + jnp.dot(weights, sens_t[pl.ds(offset, block), :], preferred_element_type=jnp.float32)
                return total

            own[0][number, there, :] = lax.fori_loop(0, nodes // span, advance, jnp.zeros((rows, sens_t.shape[1]), jnp.float32))

        start_scatter(0, number)

    def scatter_stage(level, number):
        length = lengths[level + 1]
        total = own[level][number, pl.ds(pl.multiple_of(coords[level] * length, length), length), :]
        for turn in range(1, sizes[level]):
            scatter_copy(level, number, turn).wait_recv()
            total = total + landed[level][number, turn - 1].astype(jnp.float32)
        if level + 1 < depth:
            own[level + 1][number] = total
            sent[level + 1][number] = total.astype(jnp.bfloat16)
            start_scatter(level + 1, number)
        else:
            part = pl.ds(pl.multiple_of(offsets[depth], length), length)
            gathered[number, part, :] = (total * (1.0 / 256.0)).astype(jnp.bfloat16)
            start_gather(level, number)

    def gather_stage(level, number):
        for turn in range(1, sizes[level]):
            gather_copy(level, number, turn, True).wait_recv()
        if level > 0:
            start_gather(level - 1, number)
        else:
            inverse_copy(number).wait()
            left = gathered[number].astype(jnp.float32).T.astype(jnp.bfloat16)
            part = pl.ds(pl.multiple_of(number * chunk, chunk), chunk)
            product[...] += jnp.dot(left, inverse_here[part, :], preferred_element_type=jnp.float32)

    stages = [compute]
    stages += [functools.partial(scatter_stage, level) for level in range(depth)]
    stages += [functools.partial(gather_stage, level) for level in reversed(range(depth))]

    @pl.loop(0, chunks + len(stages) - 1)
    def _(slot):
        for lag, stage in enumerate(stages):
            number = slot - lag

            @pl.when((number >= 0) & (number < chunks))
            def _():
                stage(number)

    width = final.shape[1]
    product_t[...] = product[...].T
    product_low[...] = product_t[...].astype(jnp.bfloat16)

    def final_copy(turn):
        other = lax.rem(my_ctrl + turn, ctrl_count)
        return pltpu.make_async_remote_copy(
            src_ref=product_low.at[pl.ds(pl.multiple_of(other * width, width), width), :],
            dst_ref=final.at[turn - 1],
            send_sem=final_send.at[turn - 1],
            recv_sem=final_recv.at[turn - 1],
            device_id={"ctrl": other},
            device_id_type=pl.DeviceIdType.MESH,
        )

    for turn in range(1, ctrl_count):
        final_copy(turn).start()

    @pl.loop(0, chunks)
    def _(number):
        for level, size in enumerate(sizes):
            for turn in range(1, size):
                scatter_copy(level, number, turn).wait_send()
                gather_copy(level, number, turn, False).wait_send()

    total = product_t[pl.ds(pl.multiple_of(my_ctrl * width, width), width), :]
    for turn in range(1, ctrl_count):
        final_copy(turn).wait_recv()
        total = total + final[turn - 1].astype(jnp.float32)
    out_ref[...] = total.T
    for turn in range(1, ctrl_count):
        final_copy(turn).wait_send()


def per_device(node_count, ctrl_count, sensitivity, node_xyz, ctrl_xyz, inverse):
    objs, nodes = sensitivity.shape
    ctrls, columns = inverse.shape
    sizes = level_sizes(node_count)
    chunks = max(1, min(max_chunks, ctrls // (16 * node_count)))
    chunk = ctrls // chunks
    rows, span, block = min(1024, chunk), min(2048, nodes), min(256, nodes)
    lengths = [chunk]
    for size in sizes:
        lengths.append(lengths[-1] // size)
    depth = len(sizes)
    own = [pltpu.VMEM((chunks, lengths[level], objs), jnp.float32) for level in range(depth)]
    sent_types = [jnp.float32] + [jnp.bfloat16] * (depth - 1)
    sent = [pltpu.VMEM((chunks, lengths[level], objs), jnp.bfloat16) for level in range(1, depth)]
    landed = [pltpu.VMEM((chunks, sizes[level] - 1, lengths[level + 1], objs), sent_types[level]) for level in range(depth)]
    sems = [pltpu.SemaphoreType.DMA((chunks, size - 1)) for size in sizes]

    def kernel(*refs):
        first = len(refs) - (3 * depth - 1 + 4 * depth)
        levels = list(refs[first:])
        levels.insert(depth, levels[0])
        fused_kernel(sizes, chunks, rows, span, block, *refs[:first], *levels)

    width = columns // ctrl_count
    return pl.pallas_call(
        kernel,
        out_shape=jax.ShapeDtypeStruct((objs, width), jnp.float32),
        in_specs=[pl.BlockSpec(memory_space=pltpu.VMEM)] * 3 + [pl.BlockSpec(memory_space=pl.ANY)],
        out_specs=pl.BlockSpec(memory_space=pltpu.VMEM),
        scratch_shapes=[
            pltpu.VMEM((feature_rows, nodes), jnp.float32),
            pltpu.VMEM((feature_rows, ctrls), jnp.float32),
            pltpu.VMEM((feature_rows, nodes), jnp.bfloat16),
            pltpu.VMEM((ctrls, feature_rows), jnp.bfloat16),
            pltpu.VMEM((nodes, objs), jnp.bfloat16),
            pltpu.VMEM((3, ctrls, lanes), jnp.float32),
            pltpu.VMEM((ctrls, columns), jnp.bfloat16),
            pltpu.SemaphoreType.DMA((chunks,)),
            pltpu.VMEM((chunks, chunk, objs), jnp.bfloat16),
            pltpu.VMEM((objs, columns), jnp.float32),
            pltpu.VMEM((columns, objs), jnp.float32),
            pltpu.VMEM((columns, objs), jnp.bfloat16),
            pltpu.VMEM((ctrl_count - 1, width, objs), jnp.bfloat16),
            pltpu.SemaphoreType.DMA((ctrl_count - 1,)),
            pltpu.SemaphoreType.DMA((ctrl_count - 1,)),
        ]
        + own + sent + landed + sems * 4,
        compiler_params=pltpu.CompilerParams(
            vmem_limit_bytes=56 * 2**20, collective_id=0, has_side_effects=True
        ),
    )(sensitivity, node_xyz, ctrl_xyz, inverse)


def solution(mesh):
    in_specs = (P(None, "node"), P(None, "node"), P(None, "ctrl"), P("ctrl", "node"))
    out_specs = P(None, ("node", "ctrl"))
    run = functools.partial(per_device, mesh.shape["node"], mesh.shape["ctrl"])
    return jax.shard_map(run, mesh=mesh, in_specs=in_specs, out_specs=out_specs, check_vma=False)
```
